32 devices in a mesh: seq: 16 (over z, y, core), chan: 2 (over x).
Axes of the slice: x: 2, y: 2, z: 4, core: 2. Of those that a mesh axis runs over, the one named last changes fastest.
Arguments:
- inputs: bfloat16 [2048, 8192], P('seq', 'chan'), may hold values from -256 to 256
- gating: bfloat16 [2048, 8192], P('seq', 'chan'), may hold values from -6 to 6
- long_filter: bfloat16 [513, 8192], P(None, 'chan'), may hold values from -0.25 to 0.25
- skip_scale: float32 [8192], P('chan'), may hold values from 0.5 to 1.5
Outputs:
- gated: bfloat16 [2048, 8192], P('seq', 'chan')
The draws below stay inside these ranges and needn't reach their ends.
All inputs are finite; a program needn't handle non-finite values.
Results may differ from the reference program's by a relative error of at most 0.0049.
Values may be sent and summed in bfloat16 or wider, within the bound.
No kernel may reach another device: no remote copies, remote signals or barrier semaphores. Data moves between devices by JAX's collectives and lax.ppermute only.
A program may use at most 128 MiB of HBM per device.

```python
import math
import jax
import jax.numpy as jnp
from jax import lax

D = 8192
FLEN = 513
TOKENS = 2048


def draw_inputs(key, part):
    first_key, second_key, third_key = jax.random.split(jax.random.fold_in(key, 11), 3)
    chan_pos = jnp.arange(D, dtype=jnp.float32) / max(D - 1, 1)
    rough = jnp.exp(jax.random.uniform(second_key, (1, D), jnp.float32, math.log(0.5), math.log(2.0)))
    row_scale = jnp.exp(jax.random.uniform(third_key, (TOKENS, 1), jnp.float32, 0.0, math.log(10.0)))
    column = jnp.power(10.0, 0.5 * chan_pos)[None, :]
    base = jax.random.normal(first_key, (TOKENS, D), jnp.float32)
    return jnp.clip(base * column * rough * row_scale, -256.0, 256.0).astype(jnp.bfloat16)


def shard_levels(rng, dims, pieces, least, high):
    level = 1.0
    for position, blocks in pieces:
        heights = jax.random.uniform(jax.random.fold_in(jax.random.fold_in(rng, 6), position), (blocks,), jnp.float32, least / len(pieces), high / len(pieces))
        level = level * jnp.repeat(jnp.exp(heights), dims[position] // blocks).reshape((-1,) + (1,) * (len(dims) - 1 - position))
    return level


def centred(own_key, extent, scale, reach, cuts=(), kind=jnp.bfloat16):
    factor_of = shard_levels(own_key, extent, cuts, -0.22, 0.18) if cuts else 1.0
    drawn = jax.random.normal(own_key, extent, jnp.float32) * scale * factor_of
    return jnp.minimum(jnp.maximum(drawn, -reach), reach).astype(kind)


def setup_inputs(seed: int = 0) -> dict:
    key_of = jax.random.split(jax.random.key(seed), 5)
    inputs = draw_inputs(jax.random.fold_in(key_of[4], 71), 0)
    gating = centred(key_of[1], (TOKENS, D), 1.0, 6.0, ((0, 16), (1, 2)))
    long_filter = centred(key_of[2], (FLEN, D), FLEN ** -0.5, 0.25, ((1, 2),))
    skip_scale = jnp.clip(0.5 + 1.0 * jax.random.uniform(key_of[3], (D,), jnp.float32) ** shard_levels(key_of[3], (D,), ((0, 2),), -0.2, 0.2), 0.5, 1.5)
    return dict(inputs=inputs, gating=gating, long_filter=long_filter, skip_scale=skip_scale)


def reference(inputs, gating, long_filter, skip_scale):
    values = inputs.astype(jnp.float32)
    mean_square = lax.optimization_barrier(jnp.mean(values * values, axis=1, keepdims=True))
    normed = (values * lax.rsqrt(mean_square + 1e-06)).astype(jnp.bfloat16)
    seq_length = normed.shape[0]
    tap_count = long_filter.shape[0]
    fft_size = 1 << (seq_length + tap_count - 1).bit_length()
    chan_block = min(D, 256)

    def block_conv(start):
        signal = lax.dynamic_slice_in_dim(normed, start, chan_block, 1).astype(jnp.float32)
        kernel = lax.dynamic_slice_in_dim(long_filter, start, chan_block, 1).astype(jnp.float32)
        spectrum = jnp.fft.rfft(signal, n=fft_size, axis=0) * jnp.fft.rfft(kernel, n=fft_size, axis=0)
        return jnp.fft.irfft(spectrum, n=fft_size, axis=0)[:seq_length].astype(jnp.float32)
    starts = jnp.arange(0, D, chan_block, dtype=jnp.int32)
    blocks = lax.map(block_conv, starts)
    convolved = jnp.transpose(blocks, (1, 0, 2)).reshape(seq_length, D)
    mixed = gating.astype(jnp.float32) * (convolved + skip_scale[None, :] * normed.astype(jnp.float32))
    return mixed.astype(jnp.bfloat16)
```

```python
import functools

import jax
import jax.numpy as jnp
import ml_dtypes
import numpy as np
from jax import lax
from jax.experimental import pallas as pl
from jax.experimental.pallas import tpu as pltpu
from jax.sharding import PartitionSpec as P

BF16 = jnp.bfloat16
F32 = jnp.float32
EPS = 1e-06
GROUP = 4
VMEM_LIMIT = 48 * 2**20


def split(table):
    high = table.astype(ml_dtypes.bfloat16)
    low = (table - high.astype(np.float64)).astype(ml_dtypes.bfloat16)
    return high, low


def tables(rows):
    index = np.concatenate([np.arange(0, rows, 2), np.arange(1, rows, 2)])
    turns = (index + 0.5)[:, None] * np.arange(rows)[None, :] / (2 * rows)
    angle = 2 * np.pi * turns
    forward = np.concatenate([np.cos(angle), -np.sin(angle)], 0)
    back = np.concatenate([np.cos(angle), -np.sin(angle)], 0).T / rows
    f_high, f_low = split(forward)
    b_high, b_low = split(back)
    return np.concatenate([f_high, f_low], 1), np.concatenate([b_high, b_low, b_high], 1)


def dot(left, right):
    return jnp.dot(left, right, preferred_element_type=F32)


def spectrum(table, block):
    both = dot(table, jnp.concatenate([block, block], 0))
    half = both.shape[0] // 2
    return both[:half], both[half:]


def delayed(real, imag):
    half = real.shape[0] // 2
    return (
        jnp.concatenate([-imag[:half], imag[half:]], 0),
        jnp.concatenate([real[:half], -real[half:]], 0),
    )


def plus(left, right):
    return left[0] + right[0], left[1] + right[1]


def times(left, right):
    return left[0] * right[0] - left[1] * right[1], left[0] * right[1] + left[1] * right[0]


def pick(flag, left, right):
    return jnp.where(flag, left[0], right[0]), jnp.where(flag, left[1], right[1])


def early_body(core, forward, own, far, side, taps, acc, mid, other):
    rows = own.shape[0]
    table = forward[...]
    first = core[0] == 0
    g = [spectrum(table, taps[j * rows : (j + 1) * rows, :]) for j in range(GROUP)]
    h = [g[0]] + [plus(g[j], delayed(*g[j - 1])) for j in range(1, GROUP)] + [delayed(*g[GROUP - 1])]
    total = times(spectrum(table, own[...]), h[0])
    total = plus(total, times(spectrum(table, far[...]), h[4]))
    total = plus(total, times(spectrum(table, side[...]), pick(first, h[3], h[1])))
    last = pick(first, h[1], h[3])
    for ref, value in ((acc, total), (mid, h[2]), (other, last)):
        ref[:rows, :] = value[0]
        ref[rows:, :] = value[1]


def late_body(forward, back, near, swapped, own, far, gate, scales, acc, mid, other, *rest):
    out = rest[-1]
    rows = own.shape[0]
    table = forward[...]
    total = (acc[:rows, :], acc[rows:, :])
    total = plus(total, times(spectrum(table, near[...]), (mid[:rows, :], mid[rows:, :])))
    total = plus(total, times(spectrum(table, swapped[...]), (other[:rows, :], other[rows:, :])))
    total = jnp.concatenate(total, 0)
    high = total.astype(BF16)
    low = (total - high.astype(F32)).astype(BF16)
    conv = dot(back[...], jnp.concatenate([high, high, low], 0))
    conv = conv + scales[0:1, :] * far[...].astype(F32)
    mixed = conv + scales[1:2, :] * own[...].astype(F32)
    out[...] = (gate[...].astype(F32) * mixed).astype(BF16)


def whole(array):
    return pl.BlockSpec(array.shape, lambda i: (0,) * array.ndim)


def columns(rows, tile, start=0):
    return pl.BlockSpec((rows, tile), lambda i: (0, start // tile + i))


PARAMS = pltpu.CompilerParams(vmem_limit_bytes=VMEM_LIMIT)


def early(core, forward, own, far, side, long_filter, start, tile):
    rows, width = own.shape
    spec = columns(2 * rows, tile)
    shape = jax.ShapeDtypeStruct((2 * rows, width), F32)
    return pl.pallas_call(
        early_body,
        grid=(width // tile,),
        in_specs=[pl.BlockSpec(memory_space=pltpu.SMEM), whole(forward)]
        + [columns(rows, tile)] * 3
        + [columns(GROUP * rows, tile, start)],
        out_specs=[spec] * 3,
        out_shape=[shape] * 3,
        compiler_params=PARAMS,
    )(core, forward, own, far, side, long_filter)


def late(forward, back, near, swapped, own, far, gate, scales, kept, start, tile, out):
    rows, width = own.shape
    spec = columns(2 * rows, tile)
    operands = [forward, back, near, swapped, own, far, gate, scales, *kept]
    in_specs = (
        [whole(forward), whole(back)]
        + [columns(rows, tile)] * 4
        + [columns(rows, tile, start), columns(2, tile, start)]
        + [spec] * 3
    )
    aliases = {}
    if out is not None:
        aliases = {len(operands): 0}
        operands.append(out)
        in_specs.append(pl.BlockSpec(memory_space=pl.ANY))
    return pl.pallas_call(
        late_body,
        grid=(width // tile,),
        in_specs=in_specs,
        out_specs=columns(rows, tile, start),
        out_shape=jax.ShapeDtypeStruct(gate.shape, BF16),
        input_output_aliases=aliases,
        compiler_params=PARAMS,
    )(*operands)


def shifted(value, steps):
    count = lax.axis_size("seq")
    return lax.ppermute(value, "seq", [(s, s + steps) for s in range(count - steps)])


def swapped_with(value, axis, bit):
    return lax.ppermute(value, axis, [(s, s ^ bit) for s in range(lax.axis_size(axis))])


def sum_over(value, axis):
    count = lax.axis_size(axis)
    if count & (count - 1):
        return lax.psum(value, axis)
    bit = 1
    while bit < count:
        value = value + swapped_with(value, axis, bit)
        bit *= 2
    return value


def on_device(inputs, gating, long_filter, skip_scale):
    rows, channels = inputs.shape
    place = lax.axis_index("seq")
    core = place % 2
    on_low = place // 2 % 2 == 0
    forward, back = (jnp.asarray(table) for table in tables(rows))

    values = inputs.astype(F32)
    squares = sum_over(jnp.sum(values * values, axis=1, keepdims=True), "chan")
    total_channels = channels * lax.axis_size("chan")
    normed = (values * lax.rsqrt(squares / total_channels + EPS)).astype(BF16)
    scales = jnp.stack([long_filter[-1].astype(F32), skip_scale])

    tile = channels // 8
    widths = [2 * tile, 3 * tile, 3 * tile]
    starts = [0, 2 * tile, 5 * tile]
    own = [normed[:, s : s + w] for s, w in zip(starts, widths)]
    far = [shifted(block, 4) for block in own]
    near = [swapped_with(jnp.where(on_low, own[k], far[k]), "seq", 2) for k in range(2)]
    near.append(shifted(own[2], 2))
    out = None
    core_arg = core.astype(jnp.int32).reshape(1)
    for k in range(3):
        side = swapped_with(jnp.where(core == 0, own[k], far[k]), "seq", 1)
        kept = early(core_arg, forward, own[k], far[k], side, long_filter, starts[k], tile)
        other = swapped_with(near[k], "seq", 1)
        out = late(forward, back, near[k], other, own[k], far[k], gating, scales, kept, starts[k], tile, out)
    return out


def solution(mesh):
    in_specs = (P("seq", "chan"), P("seq", "chan"), P(None, "chan"), P("chan"))
    out_specs = P("seq", "chan")
    return jax.shard_map(
        on_device, mesh=mesh, in_specs=in_specs, out_specs=out_specs, check_vma=False
    )
```

```python
import functools

import jax
import jax.numpy as jnp
import ml_dtypes
import numpy as np
from jax import lax
from jax.experimental import pallas as pl
from jax.experimental.pallas import tpu as pltpu
from jax.sharding import PartitionSpec as P

BF16 = jnp.bfloat16
F32 = jnp.float32
EPS = 1e-06
SEP = (2,)
GROUP = 4
VMEM_LIMIT = 20 * 2**20


def split(table):
    high = table.astype(ml_dtypes.bfloat16)
    low = (table - high.astype(np.float64)).astype(ml_dtypes.bfloat16)
    return high, low


def tables(rows):
    index = np.concatenate([np.arange(0, rows, 2), np.arange(1, rows, 2)])
    turns = (index + 0.5)[:, None] * np.arange(rows)[None, :] / (2 * rows)
    angle = 2 * np.pi * turns
    forward = np.concatenate([np.cos(angle), -np.sin(angle)], 0)
    back = np.concatenate([np.cos(angle), -np.sin(angle)], 0).T / rows
    f_high, f_low = split(forward)
    b_high, b_low = split(back)
    return np.concatenate([f_high, f_low], 1), np.concatenate([b_high, b_low, b_high], 1)


def dot(left, right):
    return jnp.dot(left, right, preferred_element_type=F32)


def spectrum(table, block):
    both = dot(table, jnp.concatenate([block, block], 0))
    half = both.shape[0] // 2
    return both[:half], both[half:]


def delayed(real, imag):
    half = real.shape[0] // 2
    return (
        jnp.concatenate([-imag[:half], imag[half:]], 0),
        jnp.concatenate([real[:half], -real[half:]], 0),
    )


def plus(left, right):
    return left[0] + right[0], left[1] + right[1]


def times(left, right):
    return left[0] * right[0] - left[1] * right[1], left[0] * right[1] + left[1] * right[0]


def pick(flag, left, right):
    return jnp.where(flag, left[0], right[0]), jnp.where(flag, left[1], right[1])


def store(ref, value):
    rows = value[0].shape[0]
    ref[:rows, :] = value[0]
    ref[rows:, :] = value[1]


def load(ref):
    rows = ref.shape[0] // 2
    return ref[:rows, :], ref[rows:, :]


def early_body(core, forward, own, far, *rest):
    *side, taps, total_out, side_out, near_out, swap_out = rest
    rows = own.shape[0]
    table = forward[...]
    first = core[0] == 0
    g = [spectrum(table, taps[j * rows : (j + 1) * rows, :]) for j in range(GROUP)]
    h = [g[0]] + [plus(g[j], delayed(*g[j - 1])) for j in range(1, GROUP)] + [delayed(*g[GROUP - 1])]
    total = times(spectrum(table, own[...]), h[0])
    total = plus(total, times(spectrum(table, far[...]), h[4]))
    store(total_out, total)
    store(side_out, pick(first, h[3], h[1]))
    store(near_out, h[2])
    store(swap_out, pick(first, h[1], h[3]))


def late_body(forward, back, side, near, swap, own, far, gate, scales, total_in, h_side, h_near, h_swap, *rest):
    out = rest[-1]
    table = forward[...]
    total = load(total_in)
    for block, h in ((side, h_side), (near, h_near), (swap, h_swap)):
        total = plus(total, times(spectrum(table, block[...]), load(h)))
    total = jnp.concatenate(total, 0)
    high = total.astype(BF16)
    low = (total - high.astype(F32)).astype(BF16)
    conv = dot(back[...], jnp.concatenate([high, high, low], 0))
    conv = conv + scales[0:1, :] * far[...].astype(F32)
    mixed = conv + scales[1:2, :] * own[...].astype(F32)
    out[...] = (gate[...].astype(F32) * mixed).astype(BF16)


def squares_body(x, out):
    values = x[...].astype(F32)
    total = jnp.sum(values * values, axis=1, keepdims=True)
    out[...] = jnp.broadcast_to(total, (total.shape[0], total.shape[0])).T[: out.shape[0], :]


def normed_body(total_channels, starts, x, squares, *outs):
    rows = x.shape[0]
    column = jnp.broadcast_to(squares[0:1, :], (rows, rows)).T[:, 0:1]
    factor = lax.rsqrt(column / total_channels + EPS)
    for start, out in zip(starts, outs):
        out[...] = (x[:, start : start + out.shape[1]].astype(F32) * factor).astype(BF16)


def whole(array):
    return pl.BlockSpec(array.shape, lambda i: (0,) * array.ndim)


def columns(rows, tile, start=0, block=0):
    return pl.BlockSpec((rows, tile), lambda i: (block, start // tile + i))


PARAMS = pltpu.CompilerParams(vmem_limit_bytes=VMEM_LIMIT)


def early(core, forward, own, far, long_filter, start, tile):
    rows, width = own.shape
    spec = columns(2 * rows, tile)
    shape = jax.ShapeDtypeStruct((2 * rows, width), F32)
    return pl.pallas_call(
        early_body,
        grid=(width // tile,),
        in_specs=[pl.BlockSpec(memory_space=pltpu.SMEM), whole(forward)]
        + [columns(rows, tile)] * 2
        + [columns(GROUP * rows, tile, start)],
        out_specs=[spec] * 4,
        out_shape=[shape] * 4,
        compiler_params=PARAMS,
    )(core, forward, own, far, long_filter)


def late(forward, back, side, near, swap, own, far, gate, scales, kept, start, tile, out):
    rows, width = own.shape
    operands = [forward, back, side, near, swap, own, far, gate, scales, *kept]
    in_specs = (
        [whole(forward), whole(back)]
        + [columns(rows, tile), columns(rows, tile), columns(rows, tile, 0, swap.shape[0] // rows - 1)]
        + [columns(rows, tile)] * 2
        + [columns(rows, tile, start), columns(2, tile, start)]
        + [columns(2 * rows, tile)] * 4
    )
    aliases = {}
    if out is not None:
        aliases = {len(operands): 0}
        operands.append(out)
        in_specs.append(pl.BlockSpec(memory_space=pl.ANY))
    return pl.pallas_call(
        late_body,
        grid=(width // tile,),
        in_specs=in_specs,
        out_specs=columns(rows, tile, start),
        out_shape=jax.ShapeDtypeStruct(gate.shape, BF16),
        input_output_aliases=aliases,
        compiler_params=PARAMS,
    )(*operands)


def shifted(value, steps):
    count = lax.axis_size("seq")
    return lax.ppermute(value, "seq", [(s, s + steps) for s in range(count - steps)])


def swapped_with(value, axis, bit):
    return lax.ppermute(value, axis, [(s, s ^ bit) for s in range(lax.axis_size(axis))])


def sum_over(value, axis):
    count = lax.axis_size(axis)
    if count & (count - 1):
        return lax.psum(value, axis)
    bit = 1
    while bit < count:
        value = value + swapped_with(value, axis, bit)
        bit *= 2
    return value


def on_device(inputs, gating, long_filter, skip_scale):
    rows, channels = inputs.shape
    place = lax.axis_index("seq")
    core = place % 2
    on_low = place // 2 % 2 == 0
    forward, back = (jnp.asarray(table) for table in tables(rows))

    scales = jnp.stack([long_filter[-1].astype(F32), skip_scale])

    tile = channels // 8
    widths = [3 * tile, 3 * tile, 2 * tile]
    starts = [0, 3 * tile, 6 * tile]
    squares = pl.pallas_call(
        squares_body, out_shape=jax.ShapeDtypeStruct((8, rows), F32), compiler_params=PARAMS
    )(inputs)
    squares = sum_over(squares, "chan")
    own = pl.pallas_call(
        functools.partial(normed_body, channels * lax.axis_size("chan"), starts),
        out_shape=[jax.ShapeDtypeStruct((rows, w), BF16) for w in widths],
        compiler_params=PARAMS,
    )(inputs, squares)
    own = list(own)
    far = [shifted(block, 4) for block in own]
    straight = shifted(own[2], 2)
    core_arg = core.astype(jnp.int32).reshape(1)
    tie = lax.optimization_barrier

    def begin(k):
        return early(core_arg, forward, own[k], far[k], long_filter, starts[k], tile)

    def turn(k):
        return swapped_with(jnp.where(on_low, own[k], far[k]), "seq", 2)

    def finish(k, near, out):
        side = jnp.where(core == 0, own[k], far[k])
        if k in SEP:
            side = swapped_with(side, "seq", 1)
            swap = swapped_with(near, "seq", 1)
        else:
            side = swap = swapped_with(jnp.concatenate([side, near], 0), "seq", 1)
        return late(forward, back, side, near, swap, own[k], far[k], gating, scales, kept[k], starts[k], tile, out)

    kept = [None] * 3
    near = [turn(0), None, straight]
    kept[0] = begin(0)
    far[1], kept[0] = tie((far[1], kept[0]))
    near[1] = turn(1)
    kept[1] = begin(1)
    far[2], kept[1], near[0] = tie((far[2], kept[1], near[0]))
    kept[2] = begin(2)
    near[2], kept[2] = tie((near[2], kept[2]))
    out = finish(0, near[0], None)
    out = finish(2, near[2], out)
    near[1], out = tie((near[1], out))
    out = finish(1, near[1], out)
    return out


def solution(mesh):
    in_specs = (P("seq", "chan"), P("seq", "chan"), P(None, "chan"), P("chan"))
    out_specs = P("seq", "chan")
    return jax.shard_map(
        on_device, mesh=mesh, in_specs=in_specs, out_specs=out_specs, check_vma=False
    )
```

```python
import functools

import jax
import jax.numpy as jnp
import ml_dtypes
import numpy as np
from jax import lax
from jax.experimental import pallas as pl
from jax.experimental.pallas import tpu as pltpu
from jax.sharding import PartitionSpec as P

BF16 = jnp.bfloat16
F32 = jnp.float32
EPS = 1e-06
CFG = dict(tile=256, cuts=(6, 6), g=1, hk=1, t=0, w=0, p=0, s=1, f=1)
GROUP = 4
LANES = 128
PARTS = 3
PARAMS = pltpu.CompilerParams(vmem_limit_bytes=24 * 2**20)
SMEM = pl.BlockSpec(memory_space=pltpu.SMEM)
VMEM = pl.BlockSpec(memory_space=pltpu.VMEM)
HBM = pl.BlockSpec(memory_space=pltpu.HBM)


def split(table):
    high = table.astype(ml_dtypes.bfloat16)
    low = (table - high.astype(np.float64)).astype(ml_dtypes.bfloat16)
    return high, low


def tables(rows):
    index = np.concatenate([np.arange(0, rows, 2), np.arange(1, rows, 2)])
    turns = (index + 0.5)[:, None] * np.arange(rows)[None, :] / (2 * rows)
    angle = 2 * np.pi * turns
    forward = np.concatenate([np.cos(angle), -np.sin(angle)], 0)
    back = np.concatenate([np.cos(angle), -np.sin(angle)], 0).T / rows
    f_high, f_low = split(forward)
    b_high, b_low = split(back)
    return np.concatenate([f_high, f_low], 1), np.concatenate([b_high, b_low, b_high], 1)


def dot(left, right):
    return jnp.dot(left, right, preferred_element_type=F32)


def spectrum(table, block):
    both = dot(table, jnp.concatenate([block, block], 0))
    half = both.shape[0] // 2
    return both[:half], both[half:]


def delayed(real, imag):
    half = real.shape[0] // 2
    return (
        jnp.concatenate([-imag[:half], imag[half:]], 0),
        jnp.concatenate([real[:half], -real[half:]], 0),
    )


def plus(left, right):
    return left[0] + right[0], left[1] + right[1]


def times(left, right):
    return left[0] * right[0] - left[1] * right[1], left[0] * right[1] + left[1] * right[0]


def store(ref, part, value):
    rows = value[0].shape[0]
    ref[:rows, part] = value[0]
    ref[rows:, part] = value[1]


def load(ref, part):
    rows = ref.shape[0] // 2
    return ref[:rows, part], ref[rows:, part]


def front_body(core, x, out, mine, theirs, sems):
    rows = x.shape[0]
    half = mine.shape[1]
    pieces = sems.shape[1]
    width = half // pieces

    def piece(j, k):
        side = core[0] if j == 1 else 1 - core[0]
        source = x.at[:, pl.ds(pl.multiple_of(side * half + k * width, LANES), width)]
        return pltpu.make_async_copy(source, (theirs, mine)[j].at[:, pl.ds(k * width, width)], sems.at[j, k])

    for j in range(2):
        for k in range(pieces):
            piece(j, k).start()
    total = jnp.zeros((rows, 1), F32)
    for j in range(2):
        for k in range(pieces):
            piece(j, k).wait()
            values = (theirs, mine)[j][:, k * width : (k + 1) * width].astype(F32)
            total = total + jnp.sum(values * values, axis=1, keepdims=True)
    out[...] = jnp.broadcast_to(total, (rows, rows)).T[: out.shape[0], :]


def gather_body(start, core, mine, given, out):
    rows, width = mine.shape[0], out.shape[1]
    for which in range(2):

        @pl.when(core[0] == which)
        def _():
            out[which * rows : (which + 1) * rows, :] = mine[:, start : start + width]
            out[(1 - which) * rows : (2 - which) * rows, :] = given[:, start : start + width]


def column_of(squares):
    rows = squares.shape[1]
    return jnp.broadcast_to(squares[0:1, :], (rows, rows)).T[:, 0:1]


def pack_body(total_channels, start, core, mine, given, squares, given_squares, out):
    rows = mine.shape[0]
    lane = lax.broadcasted_iota(jnp.int32, (rows, LANES), 1)
    columns = [column_of(squares), column_of(given_squares)]
    factors = [lax.rsqrt(column / total_channels + EPS) for column in columns]
    tails = []
    for left in columns:
        tail = jnp.zeros((rows, LANES), F32)
        for k in range(PARTS):
            piece = left.astype(BF16).astype(F32)
            left = left - piece
            tail = jnp.where(lane == k, piece, tail)
        tails.append(tail.astype(BF16))
    width = out.shape[1] - LANES
    for which in range(2):

        @pl.when(core[0] == which)
        def _():
            for block, factor, tail, place in zip((mine, given), factors, tails, (which, 1 - which)):
                there = slice(place * rows, (place + 1) * rows)
                out[there, :width] = (block[:, start : start + width].astype(F32) * factor).astype(BF16)
                out[there, width:] = tail


def spectra_body(tile, core, forward, taps, *rest):
    *outs, held, sems = rest
    rows = forward.shape[1] // 2
    table = forward[...]
    half = outs[0].shape[1]
    count = half // tile
    first = core[0] * half

    def fetch(k):
        source = taps.at[pl.ds(0, GROUP * rows), pl.ds(pl.multiple_of(first + k * tile, LANES), tile)]
        return pltpu.make_async_copy(source, held.at[k], sems.at[k])

    for k in range(count):
        fetch(k).start()
    for k in range(count):
        part = slice(k * tile, (k + 1) * tile)
        fetch(k).wait()
        before = None
        for j in range(GROUP):
            now = spectrum(table, held[k, j * rows : (j + 1) * rows, :])
            store(outs[j], part, now if before is None else plus(now, delayed(*before)))
            before = now
        store(outs[GROUP], part, delayed(*before))


def near_terms(near0, near1, sums, h, part):
    h1, h2, h3 = (load(h[j], part) for j in (1, 2, 3))
    sum0 = plus(sums[0], plus(times(near1, h1), times(near0, h2)))
    return sum0, plus(sums[1], plus(times(near1, h2), times(near0, h3)))


def far_terms(far0, far1, sums, h, part):
    h3, h4 = load(h[3], part), load(h[4], part)
    sum0 = plus(sums[0], plus(times(far1, h3), times(far0, h4)))
    return sum0, plus(sums[1], times(far1, h4))


def blocks(total_channels, block, part, packed):
    rows = block.shape[0] // 2
    halves = [block[j * rows : (j + 1) * rows, part] for j in range(2)]
    if packed is None:
        return halves
    begin = packed.shape[1] - LANES
    sums = sum(packed[:, begin + k : begin + k + 1].astype(F32) for k in range(PARTS))
    factor = lax.rsqrt(sums / total_channels + EPS)
    return [(half.astype(F32) * factor[j * rows : (j + 1) * rows]).astype(BF16) for j, half in enumerate(halves)]


def first_body(total_channels, tile, start, raw, forward, own, far, *rest):
    packed = rest[:2] if raw else (None, None)
    *h, sum0_out, sum1_out = rest[2:] if raw else rest
    table = forward[...]
    for k in range(sum0_out.shape[1] // tile):
        part = slice(k * tile, (k + 1) * tile)
        wide = slice(start + k * tile, start + (k + 1) * tile)
        own0, own1 = (spectrum(table, b) for b in blocks(total_channels, own, part, packed[0]))
        far0, far1 = (spectrum(table, b) for b in blocks(total_channels, far, part, packed[1]))
        same, next_ = load(h[0], wide), load(h[1], wide)
        sums = times(own0, same), plus(times(own1, same), times(own0, next_))
        sums = far_terms(far0, far1, sums, h, wide)
        store(sum0_out, part, sums[0])
        store(sum1_out, part, sums[1])


def second_body(total_channels, tile, start, raw, core, forward, back, own, far, near, *rest):
    packed = rest[:3] if raw else (None, None, None)
    last, skip, gate, given_gate, sum0, sum1, *h, own_out, given_out = rest[3:] if raw else rest
    half = gate.shape[1] // 2
    table = forward[...]
    inverse = back[...]
    first = core[0] * half + start

    def restored(total):
        total = jnp.concatenate(total, 0)
        high = total.astype(BF16)
        low = (total - high.astype(F32)).astype(BF16)
        return dot(inverse, jnp.concatenate([high, high, low], 0))

    for k in range(own_out.shape[1] // tile):
        part = slice(k * tile, (k + 1) * tile)
        local = slice(start + k * tile, start + (k + 1) * tile)
        wide = pl.ds(pl.multiple_of(first + k * tile, LANES), tile)
        near0, near1 = (spectrum(table, b) for b in blocks(total_channels, near, part, packed[2]))
        sums = near_terms(near0, near1, (load(sum0, part), load(sum1, part)), h, local)
        here, there = blocks(total_channels, own, part, packed[0]), blocks(total_channels, far, part, packed[1])
        values = []
        for j in range(2):
            value = restored(sums[j]) + last[:, wide] * there[j].astype(F32)
            values.append(value + skip[:, wide] * here[j].astype(F32))
        mine = jnp.where(core[0] == 0, values[0], values[1])
        other = jnp.where(core[0] == 0, values[1], values[0])
        own_out[:, part] = (gate[:, wide].astype(F32) * mine).astype(BF16)
        given_out[:, part] = (given_gate[:, wide].astype(F32) * other).astype(BF16)


def merge_body(starts, core, *rest):
    *parts, out, sems = rest
    half = out.shape[1] // 2
    count = len(starts)

    def move(k):
        side = core[0] if k < count else 1 - core[0]
        begin = pl.multiple_of(side * half + starts[k % count], LANES)
        return pltpu.make_async_copy(parts[k], out.at[:, pl.ds(begin, parts[k].shape[1])], sems.at[k])

    for k in range(2 * count):
        move(k).start()
    for k in range(2 * count):
        move(k).wait()


def tile_of(width):
    best = LANES
    for tile in range(LANES, CFG["tile"] + 1, LANES):
        if width % tile == 0:
            best = tile
    return best


def spectra(core, forward, taps, half):
    rows = forward.shape[1] // 2
    tile = tile_of(half)
    return pl.pallas_call(
        functools.partial(spectra_body, tile),
        in_specs=[SMEM, VMEM, HBM],
        out_specs=[VMEM] * (GROUP + 1),
        out_shape=[jax.ShapeDtypeStruct((2 * rows, half), F32)] * (GROUP + 1),
        scratch_shapes=[
            pltpu.VMEM((half // tile, GROUP * rows, tile), BF16),
            pltpu.SemaphoreType.DMA((half // tile,)),
        ],
        compiler_params=PARAMS,
    )(core, forward, taps)


def first_part(total_channels, forward, blocks, packed, h, start, width):
    operands = [forward, *blocks, *packed, *h]
    return pl.pallas_call(
        functools.partial(first_body, total_channels, tile_of(width), start, bool(packed)),
        in_specs=[VMEM] * len(operands),
        out_specs=[VMEM] * 2,
        out_shape=[jax.ShapeDtypeStruct((blocks[0].shape[0], width), F32)] * 2,
        compiler_params=PARAMS,
    )(*operands)


def second_part(total_channels, core, forward, back, blocks, packed, small, gates, sums, h, start, width):
    shape = jax.ShapeDtypeStruct((blocks[0].shape[0] // 2, width), BF16)
    operands = [core, forward, back, *blocks, *packed, *small, *gates, *sums, *h]
    return pl.pallas_call(
        functools.partial(second_body, total_channels, tile_of(width), start, bool(packed)),
        in_specs=[SMEM] + [VMEM] * (len(operands) - 1),
        out_specs=[VMEM] * 2,
        out_shape=[shape] * 2,
        compiler_params=PARAMS,
    )(*operands)


def shifted(value, steps):
    count = lax.axis_size("seq")
    return lax.ppermute(value, "seq", [(s, s + steps) for s in range(count - steps)])


def swapped_with(value, axis, bit):
    return lax.ppermute(value, axis, [(s, s ^ bit) for s in range(lax.axis_size(axis))])


def sum_over(value, axis):
    count = lax.axis_size(axis)
    if count & (count - 1):
        return lax.psum(value, axis)
    bit = 1
    while bit < count:
        value = value + swapped_with(value, axis, bit)
        bit *= 2
    return value


def on_device(inputs, gating, long_filter, skip_scale):
    rows, channels = inputs.shape
    half = channels // 2
    place = lax.axis_index("seq")
    core = place % 2
    on_low = place // 2 % 2 == 0
    core_arg = core.astype(jnp.int32).reshape(1)
    forward, back = (jnp.asarray(table) for table in tables(rows))
    tie = lax.optimization_barrier

    units = half // LANES
    cuts = [max(1, units * c // 16) for c in CFG["cuts"]]
    cuts.append(units - sum(cuts))
    cuts = [c * LANES for c in cuts]
    starts = [sum(cuts[:k]) for k in range(len(cuts))]

    inputs = pltpu.with_memory_space_constraint(inputs, pltpu.HBM)
    squares, mine, theirs = pl.pallas_call(
        front_body,
        in_specs=[SMEM, HBM],
        out_specs=[VMEM] * 3,
        out_shape=[jax.ShapeDtypeStruct((8, rows), F32)] + [jax.ShapeDtypeStruct((rows, half), BF16)] * 2,
        scratch_shapes=[pltpu.SemaphoreType.DMA((2, 2))],
        compiler_params=PARAMS,
    )(core_arg, inputs)
    given = swapped_with(theirs, "seq", 1)
    total_channels = channels * lax.axis_size("chan")

    def gathered(k, mine):
        return pl.pallas_call(
            functools.partial(gather_body, starts[k]),
            in_specs=[SMEM, VMEM, VMEM],
            out_specs=VMEM,
            out_shape=jax.ShapeDtypeStruct((2 * rows, cuts[k]), BF16),
            compiler_params=PARAMS,
        )(core_arg, mine, given)

    own = [None, None, gathered(2, mine)]
    straight = shifted(own[2], 2)
    if CFG["t"] == 2:
        squares, own[2] = tie((squares, own[2]))
    squares = sum_over(squares, "chan")
    if CFG["t"] >= 1:
        mine, squares = tie((mine, squares))
    own[0] = gathered(0, mine)
    given_squares = swapped_with(squares, "seq", 1)
    if CFG["p"]:
        given_squares, own[0] = tie((given_squares, own[0]))
    own[1] = pl.pallas_call(
        functools.partial(pack_body, total_channels, starts[1]),
        in_specs=[SMEM] + [VMEM] * 4,
        out_specs=VMEM,
        out_shape=jax.ShapeDtypeStruct((2 * rows, cuts[1] + LANES), BF16),
        compiler_params=PARAMS,
    )(core_arg, mine, given, squares, given_squares)
    if CFG["w"]:
        own[2], own[1] = tie((own[2], own[1]))
    far = [shifted(block, 4) for block in own]

    last = long_filter[GROUP * rows :].astype(F32)
    skip = skip_scale[None, :]
    taps = pltpu.with_memory_space_constraint(long_filter, pltpu.HBM)

    def turned(k):
        return swapped_with(jnp.where(on_low, own[k], far[k]), "seq", 2)

    far[0], own[1] = tie((far[0], own[1]))
    if CFG["s"]:
        far[0], straight = tie((far[0], straight))
    near = [turned(0), None, straight]
    if CFG["hk"] == 1:
        taps, far[0] = tie((taps, far[0]))
    h = spectra(core_arg, forward, taps, half)
    if CFG["hk"] == 1:
        far[1], h = tie((far[1], h))
    sent = jnp.where(on_low, own[1], far[1])
    near_rider = swapped_with(sent[:, cuts[1] :], "seq", 2)
    near[1] = swapped_with(sent[:, : cuts[1]], "seq", 2)
    if CFG["g"] == 1:
        gating, far[0] = tie((gating, far[0]))
    if CFG["g"] == 2:
        gating, far[1] = tie((gating, far[1]))
    if CFG["g"] == 3:
        gating, far[2] = tie((gating, far[2]))
    given_gate = swapped_with(gating, "seq", 1)
    if CFG["f"] == 0:
        far[0], far[1], far[2] = tie((far[0], far[1], far[2]))
    sums, made = [None] * 3, [None] * 3
    for k in range(3):
        packed = () if k == 1 else (own[1], far[1])
        sums[k] = first_part(total_channels, forward, (own[k], far[k]), packed, h, starts[k], cuts[k])
        if k < 2:
            far[k + 1], sums[k] = tie((far[k + 1], sums[k]))
    near[0], near[2], near_rider, sums[2] = tie((near[0], near[2], near_rider, sums[2]))
    order = (0, 2, 1)
    for j, k in enumerate(order):
        packed = () if k == 1 else (own[1], far[1], near_rider)
        made[k] = second_part(
            total_channels, core_arg, forward, back, (own[k], far[k], near[k]), packed,
            (last, skip), (gating, given_gate), sums[k], h, starts[k], cuts[k],
        )
        if j < 2:
            follow = order[j + 1]
            near[follow], made[k] = tie((near[follow], made[k]))
    parts = [swapped_with(part, "seq", 1) for _, part in made]
    return pl.pallas_call(
        functools.partial(merge_body, starts),
        in_specs=[SMEM] + [VMEM] * (2 * len(cuts)),
        out_specs=HBM,
        out_shape=jax.ShapeDtypeStruct(gating.shape, BF16),
        scratch_shapes=[pltpu.SemaphoreType.DMA((2 * len(cuts),))],
        compiler_params=PARAMS,
    )(core_arg, *[mine for mine, _ in made], *parts)


def solution(mesh):
    in_specs = (P("seq", "chan"), P("seq", "chan"), P(None, "chan"), P("chan"))
    out_specs = P("seq", "chan")
    return jax.shard_map(
        on_device, mesh=mesh, in_specs=in_specs, out_specs=out_specs, check_vma=False
    )
```

```python
import functools

import jax
import jax.numpy as jnp
import ml_dtypes
import numpy as np
from jax import lax
from jax.experimental import pallas as pl
from jax.experimental.pallas import tpu as pltpu
from jax.sharding import PartitionSpec as P

BF16 = jnp.bfloat16
F32 = jnp.float32
EPS = 1e-06
CFG = dict(tile=256, cuts=(6, 6), g=1, hk=1, t=0, w=0, p=0, s=1, f=1, l=0)
GROUP = 4
LANES = 128
PARTS = 3
RIDER = 16
PARAMS = pltpu.CompilerParams(vmem_limit_bytes=24 * 2**20)
SMEM = pl.BlockSpec(memory_space=pltpu.SMEM)
VMEM = pl.BlockSpec(memory_space=pltpu.VMEM)
HBM = pl.BlockSpec(memory_space=pltpu.HBM)


def split(table):
    high = table.astype(ml_dtypes.bfloat16)
    low = (table - high.astype(np.float64)).astype(ml_dtypes.bfloat16)
    return high, low


def tables(rows):
    index = np.concatenate([np.arange(0, rows, 2), np.arange(1, rows, 2)])
    turns = (index + 0.5)[:, None] * np.arange(rows)[None, :] / (2 * rows)
    angle = 2 * np.pi * turns
    forward = np.concatenate([np.cos(angle), -np.sin(angle)], 0)
    back = np.concatenate([np.cos(angle), -np.sin(angle)], 0).T / rows
    f_high, f_low = split(forward)
    b_high, b_low = split(back)
    return np.concatenate([f_high, f_low], 1), np.concatenate([b_high, b_low, b_high], 1)


def dot(left, right):
    return jnp.dot(left, right, preferred_element_type=F32)


def spectrum(table, block):
    both = dot(table, jnp.concatenate([block, block], 0))
    half = both.shape[0] // 2
    return both[:half], both[half:]


def delayed(real, imag):
    half = real.shape[0] // 2
    return (
        jnp.concatenate([-imag[:half], imag[half:]], 0),
        jnp.concatenate([real[:half], -real[half:]], 0),
    )


def plus(left, right):
    return left[0] + right[0], left[1] + right[1]


def times(left, right):
    return left[0] * right[0] - left[1] * right[1], left[0] * right[1] + left[1] * right[0]


def store(ref, part, value):
    rows = value[0].shape[0]
    ref[:rows, part] = value[0]
    ref[rows:, part] = value[1]


def load(ref, part):
    rows = ref.shape[0] // 2
    return ref[:rows, part], ref[rows:, part]


def front_body(core, x, out, mine, theirs, sems):
    rows = x.shape[0]
    half = mine.shape[1]
    pieces = sems.shape[1]
    width = half // pieces

    def piece(j, k):
        side = core[0] if j == 1 else 1 - core[0]
        source = x.at[:, pl.ds(pl.multiple_of(side * half + k * width, LANES), width)]
        return pltpu.make_async_copy(source, (theirs, mine)[j].at[:, pl.ds(k * width, width)], sems.at[j, k])

    for j in range(2):
        for k in range(pieces):
            piece(j, k).start()
    total = jnp.zeros((rows, 1), F32)
    for j in range(2):
        for k in range(pieces):
            piece(j, k).wait()
            values = (theirs, mine)[j][:, k * width : (k + 1) * width].astype(F32)
            total = total + jnp.sum(values * values, axis=1, keepdims=True)
    out[...] = jnp.broadcast_to(total, (rows, rows)).T[: out.shape[0], :]


def gather_body(start, core, mine, given, out):
    rows, width = mine.shape[0], out.shape[1]
    for which in range(2):

        @pl.when(core[0] == which)
        def _():
            out[which * rows : (which + 1) * rows, :] = mine[:, start : start + width]
            out[(1 - which) * rows : (2 - which) * rows, :] = given[:, start : start + width]


def column_of(squares):
    rows = squares.shape[1]
    return jnp.broadcast_to(squares[0:1, :], (rows, rows)).T[:, 0:1]


def pack_body(total_channels, start, core, mine, given, squares, given_squares, out):
    rows, width = mine.shape[0], out.shape[1]
    sums = (squares, given_squares)
    factors = [lax.rsqrt(column_of(s) / total_channels + EPS) for s in sums]
    line = lax.broadcasted_iota(jnp.int32, (RIDER, rows), 0)
    for which in range(2):

        @pl.when(core[0] == which)
        def _():
            tail = jnp.zeros((RIDER, rows), F32)
            for block, factor, left, place in zip((mine, given), factors, sums, (which, 1 - which)):
                part = block[:, start : start + width].astype(F32) * factor
                out[place * rows : (place + 1) * rows, :] = part.astype(BF16)
                left = left[0:1, :]
                for k in range(PARTS):
                    piece = left.astype(BF16).astype(F32)
                    left = left - piece
                    tail = jnp.where(line == place * RIDER // 2 + k, piece, tail)
            out[2 * rows :, :rows] = tail.astype(BF16)
            if width > rows:
                out[2 * rows :, rows:] = jnp.zeros((RIDER, width - rows), BF16)


def spectra_body(tile, core, forward, taps, *rest):
    *outs, held, sems = rest
    rows = forward.shape[1] // 2
    table = forward[...]
    half = outs[0].shape[1]
    count = half // tile
    first = core[0] * half

    def fetch(k):
        source = taps.at[pl.ds(0, GROUP * rows), pl.ds(pl.multiple_of(first + k * tile, LANES), tile)]
        return pltpu.make_async_copy(source, held.at[k], sems.at[k])

    for k in range(count):
        fetch(k).start()
    for k in range(count):
        part = slice(k * tile, (k + 1) * tile)
        fetch(k).wait()
        before = None
        for j in range(GROUP):
            now = spectrum(table, held[k, j * rows : (j + 1) * rows, :])
            store(outs[j], part, now if before is None else plus(now, delayed(*before)))
            before = now
        store(outs[GROUP], part, delayed(*before))


def near_terms(near0, near1, sums, h, part):
    h1, h2, h3 = (load(h[j], part) for j in (1, 2, 3))
    sum0 = plus(sums[0], plus(times(near1, h1), times(near0, h2)))
    return sum0, plus(sums[1], plus(times(near1, h2), times(near0, h3)))


def far_terms(far0, far1, sums, h, part):
    h3, h4 = load(h[3], part), load(h[4], part)
    sum0 = plus(sums[0], plus(times(far1, h3), times(far0, h4)))
    return sum0, plus(sums[1], times(far1, h4))


def blocks(total_channels, rows, block, part, packed):
    halves = [block[j * rows : (j + 1) * rows, part] for j in range(2)]
    if packed is None:
        return halves
    parts = packed[packed.shape[0] - RIDER :, :rows].astype(F32)
    outs = []
    for j, half in enumerate(halves):
        sums = sum(parts[j * RIDER // 2 + k : j * RIDER // 2 + k + 1, :] for k in range(PARTS))
        factor = lax.rsqrt(column_of(sums) / total_channels + EPS)
        outs.append((half.astype(F32) * factor).astype(BF16))
    return outs


def first_body(total_channels, tile, start, raw, forward, own, far, *rest):
    packed = rest[:2] if raw else (None, None)
    *h, sum0_out, sum1_out = rest[2:] if raw else rest
    table = forward[...]
    rows = table.shape[0] // 2
    for k in range(sum0_out.shape[1] // tile):
        part = slice(k * tile, (k + 1) * tile)
        wide = slice(start + k * tile, start + (k + 1) * tile)
        own0, own1 = (spectrum(table, b) for b in blocks(total_channels, rows, own, part, packed[0]))
        far0, far1 = (spectrum(table, b) for b in blocks(total_channels, rows, far, part, packed[1]))
        same, next_ = load(h[0], wide), load(h[1], wide)
        sums = times(own0, same), plus(times(own1, same), times(own0, next_))
        sums = far_terms(far0, far1, sums, h, wide)
        store(sum0_out, part, sums[0])
        store(sum1_out, part, sums[1])


def second_body(total_channels, tile, start, raw, core, forward, back, own, far, near, *rest):
    packed = rest[:3] if raw else (None, None, None)
    last, skip, gate, given_gate, sum0, sum1, *h, own_out, given_out = rest[3:] if raw else rest
    half = gate.shape[1] // 2
    table = forward[...]
    rows = table.shape[0] // 2
    inverse = back[...]
    first = core[0] * half + start

    def restored(total):
        total = jnp.concatenate(total, 0)
        high = total.astype(BF16)
        low = (total - high.astype(F32)).astype(BF16)
        return dot(inverse, jnp.concatenate([high, high, low], 0))

    for k in range(own_out.shape[1] // tile):
        part = slice(k * tile, (k + 1) * tile)
        local = slice(start + k * tile, start + (k + 1) * tile)
        wide = pl.ds(pl.multiple_of(first + k * tile, LANES), tile)
        near0, near1 = (spectrum(table, b) for b in blocks(total_channels, rows, near, part, packed[2]))
        sums = near_terms(near0, near1, (load(sum0, part), load(sum1, part)), h, local)
        here, there = blocks(total_channels, rows, own, part, packed[0]), blocks(total_channels, rows, far, part, packed[1])
        values = []
        for j in range(2):
            value = restored(sums[j]) + last[:, wide] * there[j].astype(F32)
            values.append(value + skip[:, wide] * here[j].astype(F32))
        mine = jnp.where(core[0] == 0, values[0], values[1])
        other = jnp.where(core[0] == 0, values[1], values[0])
        own_out[:, part] = (gate[:, wide].astype(F32) * mine).astype(BF16)
        given_out[:, part] = (given_gate[:, wide].astype(F32) * other).astype(BF16)


def merge_body(starts, core, *rest):
    *parts, out, sems = rest
    half = out.shape[1] // 2
    count = len(starts)

    def move(k):
        side = core[0] if k < count else 1 - core[0]
        begin = pl.multiple_of(side * half + starts[k % count], LANES)
        return pltpu.make_async_copy(parts[k], out.at[:, pl.ds(begin, parts[k].shape[1])], sems.at[k])

    for k in range(2 * count):
        move(k).start()
    for k in range(2 * count):
        move(k).wait()


def tile_of(width):
    best = LANES
    for tile in range(LANES, CFG["tile"] + 1, LANES):
        if width % tile == 0:
            best = tile
    return best


def spectra(core, forward, taps, half):
    rows = forward.shape[1] // 2
    tile = tile_of(half)
    return pl.pallas_call(
        functools.partial(spectra_body, tile),
        in_specs=[SMEM, VMEM, HBM],
        out_specs=[VMEM] * (GROUP + 1),
        out_shape=[jax.ShapeDtypeStruct((2 * rows, half), F32)] * (GROUP + 1),
        scratch_shapes=[
            pltpu.VMEM((half // tile, GROUP * rows, tile), BF16),
            pltpu.SemaphoreType.DMA((half // tile,)),
        ],
        compiler_params=PARAMS,
    )(core, forward, taps)


def first_part(total_channels, forward, blocks, packed, h, start, width):
    operands = [forward, *blocks, *packed, *h]
    return pl.pallas_call(
        functools.partial(first_body, total_channels, tile_of(width), start, bool(packed)),
        in_specs=[VMEM] * len(operands),
        out_specs=[VMEM] * 2,
        out_shape=[jax.ShapeDtypeStruct((forward.shape[0], width), F32)] * 2,
        compiler_params=PARAMS,
    )(*operands)


def second_part(total_channels, core, forward, back, blocks, packed, small, gates, sums, h, start, width):
    shape = jax.ShapeDtypeStruct((forward.shape[0] // 2, width), BF16)
    operands = [core, forward, back, *blocks, *packed, *small, *gates, *sums, *h]
    return pl.pallas_call(
        functools.partial(second_body, total_channels, tile_of(width), start, bool(packed)),
        in_specs=[SMEM] + [VMEM] * (len(operands) - 1),
        out_specs=[VMEM] * 2,
        out_shape=[shape] * 2,
        compiler_params=PARAMS,
    )(*operands)


def shifted(value, steps):
    count = lax.axis_size("seq")
    return lax.ppermute(value, "seq", [(s, s + steps) for s in range(count - steps)])


def swapped_with(value, axis, bit):
    return lax.ppermute(value, axis, [(s, s ^ bit) for s in range(lax.axis_size(axis))])


def sum_over(value, axis):
    count = lax.axis_size(axis)
    if count & (count - 1):
        return lax.psum(value, axis)
    bit = 1
    while bit < count:
        value = value + swapped_with(value, axis, bit)
        bit *= 2
    return value


def on_device(inputs, gating, long_filter, skip_scale):
    rows, channels = inputs.shape
    half = channels // 2
    place = lax.axis_index("seq")
    core = place % 2
    on_low = place // 2 % 2 == 0
    core_arg = core.astype(jnp.int32).reshape(1)
    forward, back = (jnp.asarray(table) for table in tables(rows))
    tie = lax.optimization_barrier

    units = half // LANES
    cuts = [max(1, units * c // 16) for c in CFG["cuts"]]
    cuts.append(units - sum(cuts))
    cuts = [c * LANES for c in cuts]
    starts = [sum(cuts[:k]) for k in range(len(cuts))]

    inputs = pltpu.with_memory_space_constraint(inputs, pltpu.HBM)
    squares, mine, theirs = pl.pallas_call(
        front_body,
        in_specs=[SMEM, HBM],
        out_specs=[VMEM] * 3,
        out_shape=[jax.ShapeDtypeStruct((8, rows), F32)] + [jax.ShapeDtypeStruct((rows, half), BF16)] * 2,
        scratch_shapes=[pltpu.SemaphoreType.DMA((2, 2))],
        compiler_params=PARAMS,
    )(core_arg, inputs)
    given = swapped_with(theirs, "seq", 1)
    total_channels = channels * lax.axis_size("chan")

    def gathered(k, mine):
        return pl.pallas_call(
            functools.partial(gather_body, starts[k]),
            in_specs=[SMEM, VMEM, VMEM],
            out_specs=VMEM,
            out_shape=jax.ShapeDtypeStruct((2 * rows, cuts[k]), BF16),
            compiler_params=PARAMS,
        )(core_arg, mine, given)

    own = [None, None, gathered(2, mine)]
    straight = shifted(own[2], 2)
    if CFG["t"] == 2:
        squares, own[2] = tie((squares, own[2]))
    squares = sum_over(squares, "chan")
    if CFG["t"] >= 1:
        mine, squares = tie((mine, squares))
    own[0] = gathered(0, mine)
    given_squares = swapped_with(squares, "seq", 1)
    if CFG["p"]:
        given_squares, own[0] = tie((given_squares, own[0]))
    own[1] = pl.pallas_call(
        functools.partial(pack_body, total_channels, starts[1]),
        in_specs=[SMEM] + [VMEM] * 4,
        out_specs=VMEM,
        out_shape=jax.ShapeDtypeStruct((2 * rows + RIDER, cuts[1]), BF16),
        compiler_params=PARAMS,
    )(core_arg, mine, given, squares, given_squares)
    if CFG["w"]:
        own[2], own[1] = tie((own[2], own[1]))
    far = [shifted(block, 4) for block in own]

    last = long_filter[GROUP * rows :].astype(F32)
    skip = skip_scale[None, :]
    taps = pltpu.with_memory_space_constraint(long_filter, pltpu.HBM)

    def turned(k):
        return swapped_with(jnp.where(on_low, own[k], far[k]), "seq", 2)

    far[0], own[1] = tie((far[0], own[1]))
    if CFG["s"]:
        far[0], straight = tie((far[0], straight))
    if CFG["l"]:
        far[0], last = tie((far[0], last))
    near = [turned(0), None, straight]
    if CFG["hk"] == 1:
        taps, far[0] = tie((taps, far[0]))
    h = spectra(core_arg, forward, taps, half)
    if CFG["hk"] == 1:
        far[1], h = tie((far[1], h))
    sent = jnp.where(on_low, own[1], far[1])
    near_rider = swapped_with(sent[2 * rows :], "seq", 2)
    near[1] = swapped_with(sent[: 2 * rows], "seq", 2)
    if CFG["g"] == 1:
        gating, far[0] = tie((gating, far[0]))
    if CFG["g"] == 2:
        gating, far[1] = tie((gating, far[1]))
    if CFG["g"] == 3:
        gating, far[2] = tie((gating, far[2]))
    given_gate = swapped_with(gating, "seq", 1)
    if CFG["f"] == 0:
        far[0], far[1], far[2] = tie((far[0], far[1], far[2]))
    sums, made = [None] * 3, [None] * 3
    for k in range(3):
        packed = () if k == 1 else (own[1], far[1])
        sums[k] = first_part(total_channels, forward, (own[k], far[k]), packed, h, starts[k], cuts[k])
        if k < 2:
            far[k + 1], sums[k] = tie((far[k + 1], sums[k]))
    near[0], near[2], near_rider, sums[2] = tie((near[0], near[2], near_rider, sums[2]))
    order = (0, 2, 1)
    for j, k in enumerate(order):
        packed = () if k == 1 else (own[1], far[1], near_rider)
        made[k] = second_part(
            total_channels, core_arg, forward, back, (own[k], far[k], near[k]), packed,
            (last, skip), (gating, given_gate), sums[k], h, starts[k], cuts[k],
        )
        if j < 2:
            follow = order[j + 1]
            near[follow], made[k] = tie((near[follow], made[k]))
    parts = [swapped_with(part, "seq", 1) for _, part in made]
    return pl.pallas_call(
        functools.partial(merge_body, starts),
        in_specs=[SMEM] + [VMEM] * (2 * len(cuts)),
        out_specs=HBM,
        out_shape=jax.ShapeDtypeStruct(gating.shape, BF16),
        scratch_shapes=[pltpu.SemaphoreType.DMA((2 * len(cuts),))],
        compiler_params=PARAMS,
    )(core_arg, *[mine for mine, _ in made], *parts)


def solution(mesh):
    in_specs = (P("seq", "chan"), P("seq", "chan"), P(None, "chan"), P("chan"))
    out_specs = P("seq", "chan")
    return jax.shard_map(
        on_device, mesh=mesh, in_specs=in_specs, out_specs=out_specs, check_vma=False
    )
```

```python
import functools

import jax
import jax.numpy as jnp
import ml_dtypes
import numpy as np
from jax import lax
from jax.experimental import pallas as pl
from jax.experimental.pallas import tpu as pltpu
from jax.sharding import PartitionSpec as P

BF16 = jnp.bfloat16
F32 = jnp.float32
EPS = 1e-06
CUTS = (5, 6)
TILE = 768
GROUP = 4
LANES = 128
PARTS = 3
RIDER = 16
PARAMS = pltpu.CompilerParams(vmem_limit_bytes=24 * 2**20)
SMEM = pl.BlockSpec(memory_space=pltpu.SMEM)
VMEM = pl.BlockSpec(memory_space=pltpu.VMEM)
HBM = pl.BlockSpec(memory_space=pltpu.HBM)


def split(table):
    high = table.astype(ml_dtypes.bfloat16)
    low = (table - high.astype(np.float64)).astype(ml_dtypes.bfloat16)
    return high, low


def tables(rows):
    index = np.concatenate([np.arange(0, rows, 2), np.arange(1, rows, 2)])
    turns = (index + 0.5)[:, None] * np.arange(rows)[None, :] / (2 * rows)
    angle = 2 * np.pi * turns
    forward = np.concatenate([np.cos(angle), -np.sin(angle)], 0)
    back = np.concatenate([np.cos(angle), -np.sin(angle)], 0).T / rows
    f_high, f_low = split(forward)
    b_high, b_low = split(back)
    return np.concatenate([f_high, f_low], 1), np.concatenate([b_high, b_low, b_high], 1)


def dot(left, right):
    return jnp.dot(left, right, preferred_element_type=F32)


def spectrum(table, block):
    both = dot(table, jnp.concatenate([block, block], 0))
    half = both.shape[0] // 2
    return both[:half], both[half:]


def delayed(real, imag):
    half = real.shape[0] // 2
    return (
        jnp.concatenate([-imag[:half], imag[half:]], 0),
        jnp.concatenate([real[:half], -real[half:]], 0),
    )


def plus(left, right):
    return left[0] + right[0], left[1] + right[1]


def times(left, right):
    return left[0] * right[0] - left[1] * right[1], left[0] * right[1] + left[1] * right[0]


def store(ref, part, value):
    rows = value[0].shape[0]
    ref[:rows, part] = value[0]
    ref[rows:, part] = value[1]


def load(ref, part):
    rows = ref.shape[0] // 2
    return ref[:rows, part], ref[rows:, part]


def front_body(core, x, out, mine, theirs, sems):
    rows = x.shape[0]
    half = mine.shape[1]
    pieces = sems.shape[1]
    width = half // pieces

    def piece(j, k):
        side = core[0] if j == 1 else 1 - core[0]
        source = x.at[:, pl.ds(pl.multiple_of(side * half + k * width, LANES), width)]
        return pltpu.make_async_copy(source, (theirs, mine)[j].at[:, pl.ds(k * width, width)], sems.at[j, k])

    for j in range(2):
        for k in range(pieces):
            piece(j, k).start()
    total = jnp.zeros((rows, 1), F32)
    for j in range(2):
        for k in range(pieces):
            piece(j, k).wait()
            values = (theirs, mine)[j][:, k * width : (k + 1) * width].astype(F32)
            total = total + jnp.sum(values * values, axis=1, keepdims=True)
    out[...] = jnp.broadcast_to(total, (rows, rows)).T[: out.shape[0], :]


def gather_body(start, core, mine, given, out):
    rows, width = mine.shape[0], out.shape[1]
    for which in range(2):

        @pl.when(core[0] == which)
        def _():
            out[which * rows : (which + 1) * rows, :] = mine[:, start : start + width]
            out[(1 - which) * rows : (2 - which) * rows, :] = given[:, start : start + width]


def column_of(squares):
    rows = squares.shape[1]
    return jnp.broadcast_to(squares[0:1, :], (rows, rows)).T[:, 0:1]


def pack_body(total_channels, start, core, mine, given, squares, given_squares, out):
    rows, width = mine.shape[0], out.shape[1]
    sums = (squares, given_squares)
    factors = [lax.rsqrt(column_of(s) / total_channels + EPS) for s in sums]
    line = lax.broadcasted_iota(jnp.int32, (RIDER, rows), 0)
    for which in range(2):

        @pl.when(core[0] == which)
        def _():
            tail = jnp.zeros((RIDER, rows), F32)
            for block, factor, left, place in zip((mine, given), factors, sums, (which, 1 - which)):
                part = block[:, start : start + width].astype(F32) * factor
                out[place * rows : (place + 1) * rows, :] = part.astype(BF16)
                left = left[0:1, :]
                for k in range(PARTS):
                    piece = left.astype(BF16).astype(F32)
                    left = left - piece
                    tail = jnp.where(line == place * RIDER // 2 + k, piece, tail)
            out[2 * rows :, :rows] = tail.astype(BF16)
            if width > rows:
                out[2 * rows :, rows:] = jnp.zeros((RIDER, width - rows), BF16)


def spectra_body(tile, core, forward, taps, *rest):
    *outs, held, sems = rest
    rows = forward.shape[1] // 2
    table = forward[...]
    half = outs[0].shape[1]
    count = half // tile
    first = core[0] * half

    def fetch(k):
        source = taps.at[pl.ds(0, GROUP * rows), pl.ds(pl.multiple_of(first + k * tile, LANES), tile)]
        return pltpu.make_async_copy(source, held.at[k], sems.at[k])

    for k in range(count):
        fetch(k).start()
    for k in range(count):
        part = slice(k * tile, (k + 1) * tile)
        fetch(k).wait()
        before = None
        for j in range(GROUP):
            now = spectrum(table, held[k, j * rows : (j + 1) * rows, :])
            store(outs[j], part, now if before is None else plus(now, delayed(*before)))
            before = now
        store(outs[GROUP], part, delayed(*before))


def near_terms(near0, near1, sums, h, part):
    h1, h2, h3 = (load(h[j], part) for j in (1, 2, 3))
    sum0 = plus(sums[0], plus(times(near1, h1), times(near0, h2)))
    return sum0, plus(sums[1], plus(times(near1, h2), times(near0, h3)))


def far_terms(far0, far1, sums, h, part):
    h3, h4 = load(h[3], part), load(h[4], part)
    sum0 = plus(sums[0], plus(times(far1, h3), times(far0, h4)))
    return sum0, plus(sums[1], times(far1, h4))


def blocks(total_channels, rows, block, part, packed):
    halves = [block[j * rows : (j + 1) * rows, part] for j in range(2)]
    if packed is None:
        return halves
    parts = packed[packed.shape[0] - RIDER :, :rows].astype(F32)
    outs = []
    for j, half in enumerate(halves):
        sums = sum(parts[j * RIDER // 2 + k : j * RIDER // 2 + k + 1, :] for k in range(PARTS))
        factor = lax.rsqrt(column_of(sums) / total_channels + EPS)
        outs.append((half.astype(F32) * factor).astype(BF16))
    return outs


def first_body(total_channels, tile, start, raw, forward, own, far, *rest):
    packed = rest[:2] if raw else (None, None)
    *h, sum0_out, sum1_out = rest[2:] if raw else rest
    table = forward[...]
    rows = table.shape[0] // 2
    for k in range(sum0_out.shape[1] // tile):
        part = slice(k * tile, (k + 1) * tile)
        wide = slice(start + k * tile, start + (k + 1) * tile)
        own0, own1 = (spectrum(table, b) for b in blocks(total_channels, rows, own, part, packed[0]))
        far0, far1 = (spectrum(table, b) for b in blocks(total_channels, rows, far, part, packed[1]))
        same, next_ = load(h[0], wide), load(h[1], wide)
        sums = times(own0, same), plus(times(own1, same), times(own0, next_))
        sums = far_terms(far0, far1, sums, h, wide)
        store(sum0_out, part, sums[0])
        store(sum1_out, part, sums[1])


def second_body(total_channels, tile, start, raw, fused, core, forward, back, own, far, near, *rest):
    packed = rest[:3] if raw else (None, None, None)
    last, skip, gate, given_gate, *rest, own_out, given_out = rest[3:] if raw else rest
    kept, h = ([], rest) if fused else (rest[:2], rest[2:])
    half = gate.shape[1] // 2
    table = forward[...]
    rows = table.shape[0] // 2
    inverse = back[...]
    first = core[0] * half + start

    def restored(total):
        total = jnp.concatenate(total, 0)
        high = total.astype(BF16)
        low = (total - high.astype(F32)).astype(BF16)
        return dot(inverse, jnp.concatenate([high, high, low], 0))

    for k in range(own_out.shape[1] // tile):
        part = slice(k * tile, (k + 1) * tile)
        local = slice(start + k * tile, start + (k + 1) * tile)
        wide = pl.ds(pl.multiple_of(first + k * tile, LANES), tile)
        near0, near1 = (spectrum(table, b) for b in blocks(total_channels, rows, near, part, packed[2]))
        here, there = (
            blocks(total_channels, rows, block, part, by) for block, by in zip((own, far), packed)
        )
        if fused:
            own0, own1, far0, far1 = (spectrum(table, block) for block in (*here, *there))
            same, next_ = load(h[0], local), load(h[1], local)
            sums = times(own0, same), plus(times(own1, same), times(own0, next_))
            sums = far_terms(far0, far1, sums, h, local)
        else:
            sums = [load(sum_, part) for sum_ in kept]
        sums = near_terms(near0, near1, sums, h, local)
        values = []
        for j in range(2):
            value = restored(sums[j]) + last[:, wide] * there[j].astype(F32)
            values.append(value + skip[:, wide] * here[j].astype(F32))
        mine = jnp.where(core[0] == 0, values[0], values[1])
        other = jnp.where(core[0] == 0, values[1], values[0])
        own_out[:, part] = (gate[:, wide].astype(F32) * mine).astype(BF16)
        given_out[:, part] = (given_gate[:, wide].astype(F32) * other).astype(BF16)


def merge_body(starts, core, *rest):
    *parts, out, sems = rest
    half = out.shape[1] // 2
    count = len(starts)

    def move(k):
        side = core[0] if k < count else 1 - core[0]
        begin = pl.multiple_of(side * half + starts[k % count], LANES)
        return pltpu.make_async_copy(parts[k], out.at[:, pl.ds(begin, parts[k].shape[1])], sems.at[k])

    for k in range(2 * count):
        move(k).start()
    for k in range(2 * count):
        move(k).wait()


def tile_of(width):
    best = LANES
    for tile in range(LANES, TILE + 1, LANES):
        if width % tile == 0:
            best = tile
    return best


def spectra(core, forward, taps, half):
    rows = forward.shape[1] // 2
    tile = tile_of(half)
    return pl.pallas_call(
        functools.partial(spectra_body, tile),
        in_specs=[SMEM, VMEM, HBM],
        out_specs=[VMEM] * (GROUP + 1),
        out_shape=[jax.ShapeDtypeStruct((2 * rows, half), F32)] * (GROUP + 1),
        scratch_shapes=[
            pltpu.VMEM((half // tile, GROUP * rows, tile), BF16),
            pltpu.SemaphoreType.DMA((half // tile,)),
        ],
        compiler_params=PARAMS,
    )(core, forward, taps)


def first_part(total_channels, forward, blocks, packed, h, start, width):
    operands = [forward, *blocks, *packed, *h]
    return pl.pallas_call(
        functools.partial(first_body, total_channels, tile_of(width), start, bool(packed)),
        in_specs=[VMEM] * len(operands),
        out_specs=[VMEM] * 2,
        out_shape=[jax.ShapeDtypeStruct((forward.shape[0], width), F32)] * 2,
        compiler_params=PARAMS,
    )(*operands)


def second_part(total_channels, core, forward, back, blocks, packed, small, gates, sums, h, start, width):
    shape = jax.ShapeDtypeStruct((forward.shape[0] // 2, width), BF16)
    operands = [core, forward, back, *blocks, *packed, *small, *gates, *sums, *h]
    return pl.pallas_call(
        functools.partial(second_body, total_channels, tile_of(width), start, bool(packed), not sums),
        in_specs=[SMEM] + [VMEM] * (len(operands) - 1),
        out_specs=[VMEM] * 2,
        out_shape=[shape] * 2,
        compiler_params=PARAMS,
    )(*operands)


def shifted(value, steps):
    count = lax.axis_size("seq")
    return lax.ppermute(value, "seq", [(s, s + steps) for s in range(count - steps)])


def swapped_with(value, axis, bit):
    return lax.ppermute(value, axis, [(s, s ^ bit) for s in range(lax.axis_size(axis))])


def sum_over(value, axis):
    count = lax.axis_size(axis)
    if count & (count - 1):
        return lax.psum(value, axis)
    bit = 1
    while bit < count:
        value = value + swapped_with(value, axis, bit)
        bit *= 2
    return value


def on_device(inputs, gating, long_filter, skip_scale):
    rows, channels = inputs.shape
    half = channels // 2
    place = lax.axis_index("seq")
    core = place % 2
    on_low = place // 2 % 2 == 0
    core_arg = core.astype(jnp.int32).reshape(1)
    forward, back = (jnp.asarray(table) for table in tables(rows))
    tie = lax.optimization_barrier

    units = half // LANES
    cuts = [max(1, units * c // 16) for c in CUTS]
    cuts.append(units - sum(cuts))
    cuts = [c * LANES for c in cuts]
    starts = [sum(cuts[:k]) for k in range(len(cuts))]

    inputs = pltpu.with_memory_space_constraint(inputs, pltpu.HBM)
    squares, mine, theirs = pl.pallas_call(
        front_body,
        in_specs=[SMEM, HBM],
        out_specs=[VMEM] * 3,
        out_shape=[jax.ShapeDtypeStruct((8, rows), F32)] + [jax.ShapeDtypeStruct((rows, half), BF16)] * 2,
        scratch_shapes=[pltpu.SemaphoreType.DMA((2, 2))],
        compiler_params=PARAMS,
    )(core_arg, inputs)
    given = swapped_with(theirs, "seq", 1)
    total_channels = channels * lax.axis_size("chan")

    def gathered(k, mine):
        return pl.pallas_call(
            functools.partial(gather_body, starts[k]),
            in_specs=[SMEM, VMEM, VMEM],
            out_specs=VMEM,
            out_shape=jax.ShapeDtypeStruct((2 * rows, cuts[k]), BF16),
            compiler_params=PARAMS,
        )(core_arg, mine, given)

    own = [None, None, gathered(2, mine)]
    straight = shifted(own[2], 2)
    squares = sum_over(squares, "chan")
    own[0] = gathered(0, mine)
    given_squares = swapped_with(squares, "seq", 1)
    own[1] = pl.pallas_call(
        functools.partial(pack_body, total_channels, starts[1]),
        in_specs=[SMEM] + [VMEM] * 4,
        out_specs=VMEM,
        out_shape=jax.ShapeDtypeStruct((2 * rows + RIDER, cuts[1]), BF16),
        compiler_params=PARAMS,
    )(core_arg, mine, given, squares, given_squares)
    far = [shifted(block, 4) for block in own]

    last = long_filter[GROUP * rows :].astype(F32)
    skip = skip_scale[None, :]
    taps = pltpu.with_memory_space_constraint(long_filter, pltpu.HBM)

    def turned(k):
        return swapped_with(jnp.where(on_low, own[k], far[k]), "seq", 2)

    far[0], own[1] = tie((far[0], own[1]))
    far[0], straight = tie((far[0], straight))
    near = [turned(0), None, straight]
    taps, far[0] = tie((taps, far[0]))
    h = spectra(core_arg, forward, taps, half)
    far[1], h = tie((far[1], h))
    sent = jnp.where(on_low, own[1], far[1])
    near_rider = swapped_with(sent[2 * rows :], "seq", 2)
    near[1] = swapped_with(sent[: 2 * rows], "seq", 2)
    gating, far[0] = tie((gating, far[0]))
    given_gate = swapped_with(gating, "seq", 1)
    sums, made = [None] * 3, [None] * 3
    for k in range(2):
        packed = () if k == 1 else (own[1], far[1])
        sums[k] = first_part(total_channels, forward, (own[k], far[k]), packed, h, starts[k], cuts[k])
        far[k + 1], sums[k] = tie((far[k + 1], sums[k]))
    sums[2] = ()
    near[0], near[2], near_rider, sums[1] = tie((near[0], near[2], near_rider, sums[1]))
    far[2], near[0] = tie((far[2], near[0]))
    order = (0, 2, 1)
    for j, k in enumerate(order):
        packed = () if k == 1 else (own[1], far[1], near_rider)
        made[k] = second_part(
            total_channels, core_arg, forward, back, (own[k], far[k], near[k]), packed,
            (last, skip), (gating, given_gate), sums[k], h, starts[k], cuts[k],
        )
        if j < 2:
            follow = order[j + 1]
            near[follow], made[k] = tie((near[follow], made[k]))
    parts = [swapped_with(part, "seq", 1) for _, part in made]
    return pl.pallas_call(
        functools.partial(merge_body, starts),
        in_specs=[SMEM] + [VMEM] * (2 * len(cuts)),
        out_specs=HBM,
        out_shape=jax.ShapeDtypeStruct(gating.shape, BF16),
        scratch_shapes=[pltpu.SemaphoreType.DMA((2 * len(cuts),))],
        compiler_params=PARAMS,
    )(core_arg, *[mine for mine, _ in made], *parts)


def solution(mesh):
    in_specs = (P("seq", "chan"), P("seq", "chan"), P(None, "chan"), P("chan"))
    out_specs = P("seq", "chan")
    return jax.shard_map(
        on_device, mesh=mesh, in_specs=in_specs, out_specs=out_specs, check_vma=False
    )
```
